32 devices in a mesh: tm: 4 (over y, core), space: 8 (over z, x).
Axes of the slice: x: 2, y: 2, z: 4, core: 2. Of those that a mesh axis runs over, the one named last changes fastest.
Arguments:
- start_field: float32 [512, 512], P('space'), may hold values from -6 to 6
- guessed: float32 [16, 512, 512], P('tm', 'space'), may hold values from -6 to 6
- diffusion: float32 [512, 512], P('space'), may hold values from 0.02 to 0.3
- peclet_x: float32 [512, 512], P('space'), may hold values from -0.9 to 0.9
- peclet_y: float32 [512, 512], P('space'), may hold values from -0.9 to 0.9
- source: float32 [512, 512], P('space'), may hold values from -0.3 to 0.3
Outputs:
- corrected: float32 [16, 512, 512], P('tm', 'space')
The draws below stay inside these ranges and needn't reach their ends.
All inputs are finite; a program needn't handle non-finite values.
Results may differ from the reference program's by a relative error of at most 0.00002.
Values sent between devices are 32-bit elements; how exact they have to be, the bound alone decides.
No kernel may reach another device: no remote copies, remote signals or barrier semaphores. Data moves between devices by JAX's collectives and lax.ppermute only.
A program may use at most 64 MiB of HBM per device.

```python
import math
import jax
import jax.numpy as jnp

COLUMNS = 512
SUBSTEPS = 4
COARSEN_ONE = 8
COARSEN_TWO = 4
SLABS = 4
C_POINTS = 16
GRID_ROWS = 512


def shard_levels(stream_key, extent, cuts, least, high):
    def one(dim, blocks):
        steps = jax.random.uniform(jax.random.fold_in(jax.random.fold_in(stream_key, 6), dim), (blocks,), jnp.float32, least / len(cuts), high / len(cuts))
        return jnp.repeat(jnp.exp(steps), extent[dim] // blocks).reshape((-1,) + (1,) * (len(extent) - dim - 1))

    loudness = one(*cuts[0])
    for cut in cuts[1:]:
        loudness = loudness * one(*cut)
    return loudness


def noise(own_key, shape, scale, reach, cuts=(), dtype=jnp.bfloat16):
    values = scale * jax.random.normal(own_key, shape, jnp.float32)
    if cuts:
        values = values * shard_levels(own_key, shape, cuts, -0.22, 0.18)
    return jnp.clip(values, -reach, reach).astype(dtype)


def setup_inputs(seed: int = 0) -> dict:
    arg_keys = jax.random.split(jax.random.key(seed), 7)
    return {
        "start_field": noise(arg_keys[0], (GRID_ROWS, COLUMNS), 1.0, 6.0, ((0, 8),), jnp.float32),
        "guessed": noise(arg_keys[1], (C_POINTS, GRID_ROWS, COLUMNS), 1.0, 6.0, ((0, 4), (1, 8)), jnp.float32),
        "diffusion": jnp.clip(jnp.exp(math.log(0.3) - 2.7080503 * jax.random.uniform(arg_keys[2], (GRID_ROWS, COLUMNS), jnp.float32) ** shard_levels(arg_keys[2], (GRID_ROWS, COLUMNS), ((0, 8),), -0.2, 0.2)), 0.02, 0.3),
        "peclet_x": jnp.clip(jax.random.uniform(arg_keys[3], (GRID_ROWS, COLUMNS), jnp.float32, -0.9, 0.9) * shard_levels(arg_keys[3], (GRID_ROWS, COLUMNS), ((0, 8),), -0.4, 0.0), -0.9, 0.9),
        "peclet_y": jnp.clip(jax.random.uniform(arg_keys[4], (GRID_ROWS, COLUMNS), jnp.float32, -0.9, 0.9) * shard_levels(arg_keys[4], (GRID_ROWS, COLUMNS), ((0, 8),), -0.4, 0.0), -0.9, 0.9),
        "source": noise(arg_keys[5], (GRID_ROWS, COLUMNS), 0.05, 0.3, ((0, 8),), jnp.float32),
    }


def substep(current, coeffs, step_scale, with_source):
    diffusion, peclet_x, peclet_y, source = coeffs
    widths = [(0, 0)] * (current.ndim - 2) + [(1, 1), (1, 1)]
    padded = jnp.pad(current, widths)
    north_row = padded[..., :-2, 1:-1]
    south_row = padded[..., 2:, 1:-1]
    west_col = padded[..., 1:-1, :-2]
    east_col = padded[..., 1:-1, 2:]
    inflow = diffusion * ((north_row + south_row + west_col + east_col) + peclet_x * (west_col - east_col) + peclet_y * (north_row - south_row))
    if with_source:
        inflow = inflow + source
    return (current + step_scale * inflow) / (1.0 + 4.0 * step_scale * diffusion)


def propagate(current, coeffs, step_scale, with_source):
    for position in range(SUBSTEPS):
        current = substep(current, coeffs, step_scale, with_source)
    return current


def reference(start_field, guessed, diffusion, peclet_x, peclet_y, source):
    coeffs = (diffusion, peclet_x, peclet_y, source)

    def relaxed(points):
        before = jnp.concatenate([start_field[None], points[:-1]], 0)
        for position in range(COARSEN_ONE):
            before = propagate(before, coeffs, 1.0, True)
        return before

    settled = relaxed(guessed)
    residual = relaxed(settled) - settled
    blocks = residual.reshape(SLABS, COARSEN_TWO, GRID_ROWS, COLUMNS)
    level_scale = float(COARSEN_ONE)
    top_scale = float(COARSEN_ONE * COARSEN_TWO)

    def coarse_step(current):
        return propagate(current, coeffs, level_scale, False)

    running = blocks[:, 0]
    for position in range(1, COARSEN_TWO):
        running = coarse_step(running) + blocks[:, position]
    c_value = running
    zero_block = jnp.zeros_like(c_value[:1])
    entering = jnp.concatenate([zero_block, c_value[:-1]], 0)
    running = entering
    for position in range(COARSEN_TWO - 1):
        running = coarse_step(running) + blocks[:, position]
    defect = (blocks[:, COARSEN_TWO - 1] + coarse_step(running)) - c_value
    running_value = jnp.zeros_like(defect[0])
    level_list = []
    for position in range(SLABS):
        running_value = propagate(running_value, coeffs, top_scale, False) + defect[position]
        level_list.append(running_value)
    c_fixed = c_value + jnp.stack(level_list, 0)
    running = jnp.concatenate([zero_block, c_fixed[:-1]], 0)
    pieces = []
    for position in range(COARSEN_TWO - 1):
        running = coarse_step(running) + blocks[:, position]
        pieces.append(running)
    pieces.append(c_fixed)
    fixed_all = jnp.stack(pieces, 1).reshape(C_POINTS, GRID_ROWS, COLUMNS)
    return settled + fixed_all
```

```python
import functools

import jax
import jax.numpy as jnp
from jax import lax
from jax.experimental import pallas as pl
from jax.experimental.pallas import tpu as pltpu
from jax.sharding import PartitionSpec as P

SUBSTEPS = 4
COARSEN_ONE = 8
COARSEN_TWO = 4
LANES = 128
PAD = 8
FAR = 16
VMEM_LIMIT = 48 * 2**20


def vmem_specs(count):
    return [pl.BlockSpec(memory_space=pltpu.VMEM)] * count


def call(kernel, name, outs, scratch, flags, *arrays, cost=0):
    return pl.pallas_call(
        kernel,
        out_shape=[jax.ShapeDtypeStruct(shape, jnp.float32) for shape in outs],
        in_specs=[pl.BlockSpec(memory_space=pltpu.SMEM)] + vmem_specs(len(arrays)),
        out_specs=vmem_specs(len(outs)),
        scratch_shapes=scratch,
        name=name,
        compiler_params=pltpu.CompilerParams(vmem_limit_bytes=VMEM_LIMIT),
        cost_estimate=pl.CostEstimate(flops=cost, bytes_accessed=1 << 20, transcendentals=0),
    )(flags, *arrays)


def column_order(columns, inverse):
    blocks = columns // LANES
    grid = lax.broadcasted_iota(jnp.int32, (columns, columns), 1 if inverse else 0)
    held = lax.broadcasted_iota(jnp.int32, (columns, columns), 0 if inverse else 1)
    matches = grid == (held % LANES) * blocks + held // LANES
    return jnp.where(matches, 1.0, 0.0).astype(jnp.bfloat16)


def split_three(value):
    high = value.astype(jnp.bfloat16)
    rest = value - high.astype(jnp.float32)
    middle = rest.astype(jnp.bfloat16)
    low = (rest - middle.astype(jnp.float32)).astype(jnp.bfloat16)
    return high, middle, low


def reorder(pieces, order):
    total = jnp.dot(pieces[2][...], order, preferred_element_type=jnp.float32)
    total = total + jnp.dot(pieces[1][...], order, preferred_element_type=jnp.float32)
    return total + jnp.dot(pieces[0][...], order, preferred_element_type=jnp.float32)


def substep(source, target, coeffs, low, high, points, with_source):
    blocks = source.shape[1]
    for row in range(low, high, 8):
        here = pl.ds(row, 8)
        centre = [[source[p, j, here, :] for j in range(blocks)] for p in range(points)]
        west_end = [pltpu.roll(centre[p][blocks - 1], 1, 1) for p in range(points)]
        east_end = [pltpu.roll(centre[p][0], LANES - 1, 1) for p in range(points)]
        for j in range(blocks):
            c = [coeffs[k, j, here, :] for k in range(6 if with_source else 5)]
            for p in range(points):
                west = west_end[p] if j == 0 else centre[p][j - 1]
                east = east_end[p] if j == blocks - 1 else centre[p][j + 1]
                north = source[p, j, pl.ds(row - 1, 8), :]
                south = source[p, j, pl.ds(row + 1, 8), :]
                own = c[0] * centre[p][j]
                if with_source:
                    own = own + c[5]
                target[p, j, here, :] = (own + (c[1] * north + c[2] * south)) + (
                    c[3] * west + c[4] * east
                )


def weights(raw, offset, coeffs, rows, scale, with_source):
    blocks = coeffs.shape[1]
    lane = lax.broadcasted_iota(jnp.int32, (8, LANES), 1)
    for j in range(blocks):
        for row in range(0, rows, 8):
            rate, along, across = (raw[k, j, pl.ds(offset + row, 8), :] for k in range(3))
            inverse = 1.0 / (1.0 + 4.0 * scale * rate)
            pull = scale * rate * inverse
            west = pull * (1.0 + along)
            east = pull * (1.0 - along)
            if j == 0:
                west = jnp.where(lane == 0, 0.0, west)
            if j == blocks - 1:
                east = jnp.where(lane == LANES - 1, 0.0, east)
            here = pl.ds(PAD + row, 8)
            coeffs[0, j, here, :] = inverse
            coeffs[1, j, here, :] = pull * (1.0 + across)
            coeffs[2, j, here, :] = pull * (1.0 - across)
            coeffs[3, j, here, :] = west
            coeffs[4, j, here, :] = east
            if with_source:
                coeffs[5, j, here, :] = scale * raw[3, j, pl.ds(offset + row, 8), :] * inverse


def clear_ends(ref):
    rows = ref.shape[2]
    edge = jnp.zeros(ref.shape[:2] + (PAD, LANES), jnp.float32)
    ref[:, :, 0:PAD, :] = edge
    ref[:, :, rows - PAD : rows, :] = edge


def arrange_kernel(flags, start, guessed, rate, along, across, drive, coeffs, late, early, first, last, *parts):
    points, rows, columns = guessed.shape
    blocks = columns // LANES
    order = column_order(columns, False)
    closing = flags[2] == 1

    @pl.when(closing)
    def _():
        for part, value in zip(parts, split_three(start[...])):
            part[pl.ds(7 * rows, rows), :] = value

    @pl.when(jnp.logical_not(closing))
    def _():
        for part, value in zip(parts, split_three(guessed[points - 1])):
            part[pl.ds(7 * rows, rows), :] = value

    fields = [rate[...], along[...], across[...], drive[...]] + [guessed[k] for k in range(points - 1)]
    for index, field in enumerate(fields):
        for part, value in zip(parts, split_three(field)):
            part[pl.ds(index * rows, rows), :] = value
    result = reorder(parts, order)
    homes = [coeffs.at[k] for k in range(4)] + [early.at[0], early.at[1], late.at[0], late.at[1]]
    for index, home in enumerate(homes):
        for j in range(blocks):
            tile = result[index * rows : (index + 1) * rows, j * LANES : (j + 1) * LANES]
            home[j] = tile
            first[index, j] = tile[:FAR]
            last[index, j] = tile[rows - FAR :]


def fill_window(even, window, base, pieces, count, shift):
    own, partner, other, above, below = pieces
    rows = own.shape[2]
    top = base + FAR
    middle = top + rows
    bottom = middle + rows
    for p in range(count):
        window[p, :, pl.ds(base, FAR), :] = above[shift + p]
        window[p, :, pl.ds(middle, rows), :] = own[p]
        window[p, :, pl.ds(bottom + rows, FAR), :] = below[shift + p]

        @pl.when(even)
        def _():
            window[p, :, pl.ds(top, rows), :] = other[p]
            window[p, :, pl.ds(bottom, rows), :] = partner[p]

        @pl.when(jnp.logical_not(even))
        def _():
            window[p, :, pl.ds(top, rows), :] = partner[p]
            window[p, :, pl.ds(bottom, rows), :] = other[p]


def run_sweeps(a, b, coeffs, rows, points, snapshot):
    half = SUBSTEPS * COARSEN_ONE
    for stage in range(2 * half // 8):
        if stage == half // 8:
            snapshot()
        low = PAD + 8 * stage
        high = PAD + rows - 8 * stage

        def pair(_, carry):
            substep(a, b, coeffs, low, high, points, True)
            substep(b, a, coeffs, low, high, points, True)
            return carry

        lax.fori_loop(0, 4, pair, 0)


def late_kernel(flags, c0, c1, c2, above, below, f0, f1, f2, shift_out, settled_out, raw_out, raw, coeffs, a, b):
    even = flags[1] == 0
    rows = c0.shape[2]
    total = 3 * rows + 2 * FAR
    fill_window(even, raw, 0, (c0, c1, c2, above, below), 4, 0)
    weights(raw, 0, coeffs, total, 1.0, True)
    raw_rows = raw_out.shape[2]
    raw_out[...] = raw[0:3, :, pl.ds((total - raw_rows) // 2, raw_rows), :]
    for ref in (a, b):
        clear_ends(ref)
    fill_window(even, a, PAD, (f0, f1, f2, above, below), 2, 6)
    kept = rows + 2 * FAR
    keep = pl.ds(PAD + 2 * SUBSTEPS * COARSEN_ONE, kept)

    def snapshot():
        settled_out[...] = a[0, :, keep, :]
        shift_out[2] = a[1, :, keep, :]

    run_sweeps(a, b, coeffs, total, 2, snapshot)
    shift_out[1] = a[1, :, keep, :]

    @pl.when(flags[2] == 1)
    def _():
        shift_out[0] = shift_out[2] - shift_out[2]

    @pl.when(flags[2] == 0)
    def _():
        shift_out[0] = a[0, :, keep, :] - shift_out[2]


def early_kernel(flags, c0, c1, c2, above, below, f0, f1, f2, settled_out, swept_out, raw, coeffs, a, b):
    even = flags[1] == 0
    rows = c0.shape[2]
    total = 3 * rows + 2 * FAR
    fill_window(even, raw, 0, (c0, c1, c2, above, below), 4, 0)
    weights(raw, 0, coeffs, total, 1.0, True)
    for ref in (a, b):
        clear_ends(ref)
    fill_window(even, a, PAD, (f0, f1, f2, above, below), 2, 4)
    keep = pl.ds(PAD + 2 * SUBSTEPS * COARSEN_ONE, rows + 2 * FAR)

    def snapshot():
        settled_out[...] = a[:, :, keep, :]

    run_sweeps(a, b, coeffs, total, 2, snapshot)
    swept_out[...] = a[:, :, keep, :]


def coarse_step(a, b, coeffs, low, high, points):
    for _ in range(SUBSTEPS // 2):
        substep(a, b, coeffs, low, high, points, False)
        substep(b, a, coeffs, low, high, points, False)


def slab_kernel(flags, raw, arrived, settled, swept, settled_last, e_out, c_out, coeffs, a, b):
    kept = settled.shape[2]
    rows = kept - 2 * FAR
    weights(raw, (raw.shape[2] - kept) // 2, coeffs, kept, float(COARSEN_ONE), False)
    for ref in (a, b):
        clear_ends(ref)
    own = pl.ds(FAR, rows)
    residual = [
        lambda: arrived[0],
        lambda: arrived[1] - settled[0],
        lambda: swept[0] - settled[1],
        lambda: swept[1] - settled_last[...],
    ]
    inner = pl.ds(PAD, kept)
    a[0, :, inner, :] = residual[0]()
    e_out[0] = a[0, :, pl.ds(PAD + FAR, rows), :]
    for position in range(1, COARSEN_TWO):
        trim = 8 * ((position - 1) * SUBSTEPS // 8)
        coarse_step(a, b, coeffs, PAD + trim, PAD + kept - trim, 1)
        a[0, :, inner, :] = a[0, :, inner, :] + residual[position]()
        e_out[position] = a[0, :, pl.ds(PAD + FAR, rows), :]
    c_out[...] = e_out[COARSEN_TWO - 1]


def close_kernel(flags, raw, gathered, edges, arrived, settled, settled_last, e, out, level_coeffs, top_coeffs, a, b, w, l, x, y, *parts):
    slabs = gathered.shape[0]
    chain = slabs - 1
    rows = gathered.shape[2]
    reach = edges.shape[3]
    total = rows + 2 * reach
    offset = (raw.shape[2] - total) // 2
    weights(raw, offset, level_coeffs, total, float(COARSEN_ONE), False)
    weights(raw, offset, top_coeffs, total, float(COARSEN_ONE * COARSEN_TWO), False)
    for ref in (a, b, x, y):
        clear_ends(ref)
    for k in range(chain):
        a[k, :, pl.ds(PAD, reach), :] = edges[k, 0]
        a[k, :, pl.ds(PAD + reach, rows), :] = gathered[k]
        a[k, :, pl.ds(PAD + reach + rows, reach), :] = edges[k, 1]
    inner = pl.ds(PAD, total)
    w[0] = jnp.zeros(w.shape[1:], jnp.float32)
    l[0] = jnp.zeros(l.shape[1:], jnp.float32)
    for k in range(chain):
        w[k + 1] = a[k, :, inner, :]
    for step in range(COARSEN_TWO):
        trim = 8 * (step * SUBSTEPS // 8)
        coarse_step(a, b, level_coeffs, PAD + trim, PAD + total - trim, chain)
    used = COARSEN_TWO * SUBSTEPS
    x[0, :, inner, :] = a[0, :, inner, :]
    l[1] = x[0, :, inner, :]
    for k in range(1, chain):
        w[k + 1] = w[k + 1] + l[k]
        trim = 8 * (used // 8)
        coarse_step(x, y, top_coeffs, PAD + trim, PAD + total - trim, 1)
        used += SUBSTEPS
        x[0, :, inner, :] = x[0, :, inner, :] + a[k, :, inner, :]
        l[k + 1] = x[0, :, inner, :]
    slab = flags[0]
    own = pl.ds(reach, rows)
    held = pl.ds(PAD + reach, rows)
    x[0, :, inner, :] = w[slab]
    settled_own = pl.ds(FAR, rows)
    blocks = gathered.shape[1]
    for position in range(COARSEN_TWO):
        if position < COARSEN_TWO - 1:
            trim = 8 * ((reach - COARSEN_TWO * SUBSTEPS + SUBSTEPS * position) // 8)
            coarse_step(x, y, level_coeffs, PAD + trim, PAD + total - trim, 1)
            settled_here = arrived.at[2] if position == 0 else settled.at[position - 1]
            value = x[0, :, held, :]
        else:
            settled_here = settled_last
            value = l[slab, :, own, :]
        value = (settled_here[:, settled_own, :] + e[position]) + value
        for j in range(blocks):
            for part, piece in zip(parts, split_three(value[j])):
                part[pl.ds(position * rows, rows), j * LANES : (j + 1) * LANES] = piece
    result = reorder(parts, column_order(blocks * LANES, True))
    for position in range(COARSEN_TWO):
        out[position] = result[position * rows : (position + 1) * rows]


def on_device(start_field, guessed, diffusion, peclet_x, peclet_y, source):
    points, rows, columns = guessed.shape
    blocks = columns // LANES
    slab = lax.axis_index("tm")
    slabs = lax.axis_size("tm")
    strip = lax.axis_index("space")
    strips = lax.axis_size("space")
    flags = jnp.stack([slab, strip % 2, (slab == slabs - 1).astype(jnp.int32)]).astype(jnp.int32)

    field = (blocks, rows, LANES)
    parts = [pltpu.VMEM((8 * rows, columns), jnp.bfloat16)] * 3
    coeffs, late, early, first, last = call(
        arrange_kernel, "arrange",
        [(4,) + field, (2,) + field, (2,) + field, (8, blocks, FAR, LANES), (8, blocks, FAR, LANES)],
        parts, flags, start_field, guessed, diffusion, peclet_x, peclet_y, source,
    )
    swap = [(i, i ^ 1) for i in range(strips)]
    up = [(i, i + 2) for i in range(strips - 2)]
    down = [(i + 2, i) for i in range(strips - 2)]
    onward = [(i, i + 2) for i in range(0, strips - 2, 2)] + [(i, i - 2) for i in range(3, strips, 2)]

    above = lax.ppermute(last, "space", up)
    below = lax.ppermute(first, "space", down)
    coeffs_partner = lax.ppermute(coeffs, "space", swap)
    late_partner = lax.ppermute(late, "space", swap)
    early_partner = lax.ppermute(early, "space", swap)
    coeffs_other = lax.ppermute(coeffs_partner, "space", onward)
    late_other = lax.ppermute(late_partner, "space", onward)
    early_other = lax.ppermute(early_partner, "space", onward)

    total = 3 * rows + 2 * FAR
    kept = rows + 2 * FAR
    reach = 8 * -(-(SUBSTEPS * (2 * COARSEN_TWO - 1 + max(slabs - 3, 0))) // 8)
    spread = max(reach, FAR)
    window = (blocks, total + 2 * PAD, LANES)
    scratch = [
        pltpu.VMEM((4, blocks, total, LANES), jnp.float32),
        pltpu.VMEM((6,) + window, jnp.float32),
        pltpu.VMEM((2,) + window, jnp.float32),
        pltpu.VMEM((2,) + window, jnp.float32),
    ]
    work = 2 * SUBSTEPS * COARSEN_ONE * 2 * 10 * columns * (total - 56)
    near = (blocks, kept, LANES)
    outgoing, settled_last, raw = call(
        late_kernel, "late_points",
        [(3,) + near, near, (3, blocks, rows + 2 * spread, LANES)], scratch, flags,
        coeffs, coeffs_partner, coeffs_other, above, below, late, late_partner, late_other, cost=work,
    )
    arrived = lax.ppermute(outgoing, "tm", [(i, (i + 1) % slabs) for i in range(slabs)])
    settled, swept = call(
        early_kernel, "early_points", [(2,) + near, (2,) + near], scratch, flags,
        coeffs, coeffs_partner, coeffs_other, above, below, early, early_partner, early_other, cost=work,
    )
    padded = (blocks, kept + 2 * PAD, LANES)
    e, c_value = call(
        slab_kernel, "slab_value", [(COARSEN_TWO,) + field, field],
        [pltpu.VMEM((5,) + padded, jnp.float32)] + [pltpu.VMEM((1,) + padded, jnp.float32)] * 2,
        flags, raw, arrived, settled, swept, settled_last,
    )
    forward = [(i, i + 1) for i in range(strips - 1)]
    backward = [(i + 1, i) for i in range(strips - 1)]
    from_above = lax.ppermute(c_value[:, rows - reach :, :], "space", forward)
    from_below = lax.ppermute(c_value[:, :reach, :], "space", backward)
    gathered = lax.all_gather(c_value, "tm")
    edges = lax.all_gather(jnp.stack([from_above, from_below]), "tm")

    span = rows + 2 * reach
    wide = (blocks, span + 2 * PAD, LANES)
    plain = (slabs, blocks, span, LANES)
    out_parts = [pltpu.VMEM((COARSEN_TWO * rows, columns), jnp.bfloat16)] * 3
    (out,) = call(
        close_kernel, "close", [(COARSEN_TWO, rows, columns)],
        [pltpu.VMEM((5,) + wide, jnp.float32)] * 2
        + [pltpu.VMEM((slabs - 1,) + wide, jnp.float32)] * 2
        + [pltpu.VMEM(plain, jnp.float32)] * 2
        + [pltpu.VMEM((1,) + wide, jnp.float32)] * 2
        + out_parts,
        flags, raw, gathered, edges, arrived, settled, settled_last, e,
    )
    return out


def solution(mesh):
    in_specs = (
        P("space", None),
        P("tm", "space", None),
        P("space", None),
        P("space", None),
        P("space", None),
        P("space", None),
    )
    out_specs = P("tm", "space", None)
    return jax.shard_map(
        on_device, mesh=mesh, in_specs=in_specs, out_specs=out_specs, check_vma=False
    )
```

```python
import functools

import jax
import jax.numpy as jnp
from jax import lax
from jax.experimental import pallas as pl
from jax.experimental.pallas import tpu as pltpu
from jax.sharding import PartitionSpec as P

SUBSTEPS = 4
COARSEN_ONE = 8
COARSEN_TWO = 4
LANES = 128
PAD = 8
NEAR = 16
FINE = SUBSTEPS * COARSEN_ONE
VMEM_LIMIT = 24 * 2**20


def is_last_slab():
    return lax.axis_index("tm") == lax.axis_size("tm") - 1


def vmem_specs(count):
    return [pl.BlockSpec(memory_space=pltpu.VMEM)] * count


def call(kernel, name, outs, scratch, *arrays, cost=0, far=False, grant=VMEM_LIMIT):
    held = [pl.BlockSpec(memory_space=pltpu.HBM)] * len(arrays) if far else vmem_specs(len(arrays))
    return pl.pallas_call(
        kernel,
        out_shape=[jax.ShapeDtypeStruct(shape, jnp.float32) for shape in outs],
        in_specs=held,
        out_specs=vmem_specs(len(outs)),
        scratch_shapes=scratch,
        name=name,
        compiler_params=pltpu.CompilerParams(vmem_limit_bytes=grant),
        cost_estimate=pl.CostEstimate(flops=cost, bytes_accessed=1 << 20, transcendentals=0),
    )(*arrays)


def column_order(columns, inverse):
    blocks = columns // LANES
    grid = lax.broadcasted_iota(jnp.int32, (columns, columns), 1 if inverse else 0)
    held = lax.broadcasted_iota(jnp.int32, (columns, columns), 0 if inverse else 1)
    matches = grid == (held % LANES) * blocks + held // LANES
    return jnp.where(matches, 1.0, 0.0).astype(jnp.bfloat16)


def split_three(value):
    high = value.astype(jnp.bfloat16)
    rest = value - high.astype(jnp.float32)
    middle = rest.astype(jnp.bfloat16)
    low = (rest - middle.astype(jnp.float32)).astype(jnp.bfloat16)
    return high, middle, low


def reorder(pieces, order):
    total = jnp.dot(pieces[2][...], order, preferred_element_type=jnp.float32)
    total = total + jnp.dot(pieces[1][...], order, preferred_element_type=jnp.float32)
    return total + jnp.dot(pieces[0][...], order, preferred_element_type=jnp.float32)


def substep(source, target, coeffs, low, high, points, with_source):
    blocks = source.shape[1]
    for row in range(low, high, 8):
        here = pl.ds(row, 8)
        centre = [[source[p, j, here, :] for j in range(blocks)] for p in range(points)]
        west_end = [pltpu.roll(centre[p][blocks - 1], 1, 1) for p in range(points)]
        east_end = [pltpu.roll(centre[p][0], LANES - 1, 1) for p in range(points)]
        for j in range(blocks):
            c = [coeffs[k, j, here, :] for k in range(6 if with_source else 5)]
            for p in range(points):
                west = west_end[p] if j == 0 else centre[p][j - 1]
                east = east_end[p] if j == blocks - 1 else centre[p][j + 1]
                north = source[p, j, pl.ds(row - 1, 8), :]
                south = source[p, j, pl.ds(row + 1, 8), :]
                own = c[0] * centre[p][j]
                if with_source:
                    own = own + c[5]
                target[p, j, here, :] = (own + (c[1] * north + c[2] * south)) + (
                    c[3] * west + c[4] * east
                )


def weights(raw, offset, coeffs, rows, scale, with_source):
    blocks = coeffs.shape[1]
    lane = lax.broadcasted_iota(jnp.int32, (8, LANES), 1)
    for j in range(blocks):
        for row in range(0, rows, 8):
            rate, along, across = (raw[k, j, pl.ds(offset + row, 8), :] for k in range(3))
            inverse = 1.0 / (1.0 + 4.0 * scale * rate)
            pull = scale * rate * inverse
            west = pull * (1.0 + along)
            east = pull * (1.0 - along)
            if j == 0:
                west = jnp.where(lane == 0, 0.0, west)
            if j == blocks - 1:
                east = jnp.where(lane == LANES - 1, 0.0, east)
            here = pl.ds(PAD + row, 8)
            coeffs[0, j, here, :] = inverse
            coeffs[1, j, here, :] = pull * (1.0 + across)
            coeffs[2, j, here, :] = pull * (1.0 - across)
            coeffs[3, j, here, :] = west
            coeffs[4, j, here, :] = east
            if with_source:
                coeffs[5, j, here, :] = scale * raw[3, j, pl.ds(offset + row, 8), :] * inverse


def clear_ends(ref):
    rows = ref.shape[2]
    edge = jnp.zeros(ref.shape[:2] + (PAD, LANES), jnp.float32)
    ref[:, :, 0:PAD, :] = edge
    ref[:, :, rows - PAD : rows, :] = edge


def sides(source, near, far):
    even = lax.axis_index("space") % 2 == 0
    rows = source.shape[-2]
    width = near.shape[-2]
    low = pl.multiple_of(jnp.where(even, rows - width, 0), 8)
    high = pl.multiple_of(jnp.where(even, 0, rows - width), 8)
    for k in range(near.shape[0]):
        near[k] = source[k, :, pl.ds(low, width), :]
        far[k] = source[k, :, pl.ds(high, width), :]


def arrange_kernel(
    start, guessed, rate, along, across, drive,
    coeffs, late, early, share_near, share_far, late_near, late_far, early_near, early_far,
    landed, arrivals, *parts,
):
    points, rows, columns = guessed.shape
    blocks = columns // LANES
    closing = is_last_slab()
    sources = [rate, along, across, drive] + [guessed.at[k] for k in range(points - 1)]
    copies = [
        pltpu.make_async_copy(source, landed.at[k], arrivals.at[k]) for k, source in enumerate(sources)
    ]
    final = [
        pltpu.make_async_copy(source, landed.at[7], arrivals.at[7]) for source in (start, guessed.at[points - 1])
    ]
    for copy in copies:
        copy.start()

    @pl.when(closing)
    def _():
        final[0].start()

    @pl.when(jnp.logical_not(closing))
    def _():
        final[1].start()

    order = column_order(columns, False)
    for index, copy in enumerate(copies + final[1:]):
        copy.wait()
        for part, value in zip(parts, split_three(landed[index])):
            part[pl.ds(index * rows, rows), :] = value
    result = reorder(parts, order)
    homes = [coeffs.at[k] for k in range(4)] + [early.at[0], early.at[1], late.at[0], late.at[1]]
    for index, home in enumerate(homes):
        for j in range(blocks):
            home[j] = result[index * rows : (index + 1) * rows, j * LANES : (j + 1) * LANES]
    sides(coeffs.at[pl.ds(2 * (lax.axis_index("tm") % 2), 2)], share_near, share_far)
    sides(late, late_near, late_far)
    sides(early, early_near, early_far)


def fill(window, base, own, near, far, targets):
    even = lax.axis_index("space") % 2 == 0
    rows = own.shape[2]
    width = near.shape[2]
    below = base + width + rows
    partner = pl.multiple_of(jnp.where(even, below, base), 8)
    other = pl.multiple_of(jnp.where(even, base, below), 8)
    for k, target in enumerate(targets):
        window[target, :, pl.ds(partner, width), :] = near[k]
        window[target, :, pl.ds(other, width), :] = far[k]


def run_sweep(a, b, coeffs, base, rows, points):
    for stage in range(FINE // 8):
        low = base + 8 * stage
        high = base + rows - 8 * stage

        def pairs(_, carry):
            for _ in range(2):
                substep(a, b, coeffs, low, high, points, True)
                substep(b, a, coeffs, low, high, points, True)
            return carry

        lax.fori_loop(0, 2, pairs, 0)


def load_points(a, b, own, near, far):
    points, _, rows, _ = own.shape
    width = near.shape[2]
    base = (a.shape[2] - rows) // 2 - width
    total = rows + 2 * width
    edge = jnp.zeros(a.shape[:2] + (PAD, LANES), jnp.float32)
    for ref in (a, b):
        ref[:, :, pl.ds(base - PAD, PAD), :] = edge
        ref[:, :, pl.ds(base + total, PAD), :] = edge
    for p in range(points):
        a[p, :, pl.ds(base + width, rows), :] = own[p]
    fill(a, base, own, near, far, range(points))
    return base, total


def first_sweep(coeffs, own, near, far, settled, next_near, next_far, a, b):
    base, total = load_points(a, b, own, near, far)
    run_sweep(a, b, coeffs, base, total, own.shape[0])
    settled[...] = a[:, :, pl.ds(base + FINE, own.shape[2]), :]
    sides(settled, next_near, next_far)


def open_kernel(
    mine, share_near, share_far, mates, own, near, far,
    coeffs, raw_out, settled, next_near, next_far, raw, a, b,
):
    rows = mine.shape[2]
    width = share_near.shape[2]
    total = rows + 2 * width
    for k in range(4):
        raw[k, :, pl.ds(width, rows), :] = mine[k]
    fill(raw, 0, mine, share_near, share_far, [2 * (lax.axis_index("tm") % 2) + k for k in range(2)])
    fill(raw, 0, mine, mates.at[0], mates.at[1], [2 - 2 * (lax.axis_index("tm") % 2) + k for k in range(2)])
    weights(raw, 0, coeffs, total, 1.0, True)
    clear_ends(coeffs)
    raw_rows = raw_out.shape[2]
    raw_out[...] = raw[0:3, :, pl.ds((total - raw_rows) // 2, raw_rows), :]
    first_sweep(coeffs, own, near, far, settled, next_near, next_far, a, b)


def second_sweep(coeffs, own, near, far, a, b):
    base, total = load_points(a, b, own, near, far)
    keep = pl.ds(base + FINE, total - 2 * FINE)
    return base, total, keep


def late_kernel(coeffs, own, near, far, shift_out, a, b):
    base, total, keep = second_sweep(coeffs, own, near, far, a, b)
    shift_out[2] = a[1, :, keep, :]
    run_sweep(a, b, coeffs, base, total, own.shape[0])
    shift_out[1] = a[1, :, keep, :]

    @pl.when(is_last_slab())
    def _():
        shift_out[0] = shift_out[2] - shift_out[2]

    @pl.when(jnp.logical_not(is_last_slab()))
    def _():
        shift_out[0] = a[0, :, keep, :] - shift_out[2]


def early_kernel(coeffs, own, near, far, settled_out, swept_out, a, b):
    base, total, keep = second_sweep(coeffs, own, near, far, a, b)
    settled_out[...] = a[:, :, keep, :]
    run_sweep(a, b, coeffs, base, total, own.shape[0])
    swept_out[...] = a[:, :, keep, :]


def coarse_step(a, b, coeffs, low, high, points):
    for _ in range(SUBSTEPS // 2):
        substep(a, b, coeffs, low, high, points, False)
        substep(b, a, coeffs, low, high, points, False)


def slab_kernel(raw, arrived, settled, swept, settled_last, e_out, c_out, coeffs, a, b):
    kept = settled.shape[2]
    rows = settled_last.shape[2]
    weights(raw, (raw.shape[2] - kept) // 2, coeffs, kept, float(COARSEN_ONE), False)
    for ref in (a, b):
        clear_ends(ref)
    inner = pl.ds(PAD, kept)
    own = pl.ds(NEAR, rows)
    held = pl.ds(PAD + NEAR, rows)
    a[0, :, inner, :] = arrived[0]
    e_out[0] = a[0, :, held, :]
    for position in range(1, COARSEN_TWO):
        trim = 8 * ((position - 1) * SUBSTEPS // 8)
        coarse_step(a, b, coeffs, PAD + trim, PAD + kept - trim, 1)
        if position == 1:
            a[0, :, inner, :] = a[0, :, inner, :] + (arrived[1] - settled[0])
        elif position == 2:
            a[0, :, inner, :] = a[0, :, inner, :] + (swept[0] - settled[1])
        else:
            a[0, :, held, :] = a[0, :, held, :] + (swept[1, :, own, :] - settled_last[0])
        e_out[position] = a[0, :, held, :]
    c_out[...] = e_out[COARSEN_TWO - 1]


def close_kernel(raw, gathered, edges, arrived, settled, settled_last, e, out, level_coeffs, top_coeffs, a, b, w, l, x, y, *parts):
    slabs = gathered.shape[0]
    chain = slabs - 1
    rows = gathered.shape[2]
    reach = edges.shape[3]
    total = rows + 2 * reach
    offset = (raw.shape[2] - total) // 2
    weights(raw, offset, level_coeffs, total, float(COARSEN_ONE), False)
    weights(raw, offset, top_coeffs, total, float(COARSEN_ONE * COARSEN_TWO), False)
    for ref in (a, b, x, y):
        clear_ends(ref)
    for k in range(chain):
        a[k, :, pl.ds(PAD, reach), :] = edges[k, 0]
        a[k, :, pl.ds(PAD + reach, rows), :] = gathered[k]
        a[k, :, pl.ds(PAD + reach + rows, reach), :] = edges[k, 1]
    inner = pl.ds(PAD, total)
    w[0] = jnp.zeros(w.shape[1:], jnp.float32)
    l[0] = jnp.zeros(l.shape[1:], jnp.float32)
    for k in range(chain):
        w[k + 1] = a[k, :, inner, :]
    for step in range(COARSEN_TWO):
        trim = 8 * (step * SUBSTEPS // 8)
        coarse_step(a, b, level_coeffs, PAD + trim, PAD + total - trim, chain)
    used = COARSEN_TWO * SUBSTEPS
    x[0, :, inner, :] = a[0, :, inner, :]
    l[1] = x[0, :, inner, :]
    for k in range(1, chain):
        w[k + 1] = w[k + 1] + l[k]
        trim = 8 * (used // 8)
        coarse_step(x, y, top_coeffs, PAD + trim, PAD + total - trim, 1)
        used += SUBSTEPS
        x[0, :, inner, :] = x[0, :, inner, :] + a[k, :, inner, :]
        l[k + 1] = x[0, :, inner, :]
    slab = lax.axis_index("tm")
    own = pl.ds(reach, rows)
    held = pl.ds(PAD + reach, rows)
    x[0, :, inner, :] = w[slab]
    blocks = gathered.shape[1]
    for position in range(COARSEN_TWO):
        if position < COARSEN_TWO - 1:
            trim = 8 * ((reach - COARSEN_TWO * SUBSTEPS + SUBSTEPS * position) // 8)
            coarse_step(x, y, level_coeffs, PAD + trim, PAD + total - trim, 1)
            settled_here = (arrived.at[2] if position == 0 else settled.at[position - 1]).at[:, pl.ds(NEAR, rows), :]
            value = x[0, :, held, :]
        else:
            settled_here = settled_last.at[0]
            value = l[slab, :, own, :]
        value = (settled_here[...] + e[position]) + value
        for j in range(blocks):
            for part, piece in zip(parts, split_three(value[j])):
                part[pl.ds(position * rows, rows), j * LANES : (j + 1) * LANES] = piece
    result = reorder(parts, column_order(blocks * LANES, True))
    for position in range(COARSEN_TWO):
        out[position] = result[position * rows : (position + 1) * rows]


def on_device(start_field, guessed, diffusion, peclet_x, peclet_y, source):
    points, rows, columns = guessed.shape
    blocks = columns // LANES
    slabs = lax.axis_size("tm")
    strips = lax.axis_size("space")

    field = (blocks, rows, LANES)
    parts = [pltpu.VMEM((8 * rows, columns), jnp.bfloat16)] * 3
    landing = [pltpu.VMEM((8, rows, columns), jnp.float32), pltpu.SemaphoreType.DMA((8,))]
    wide_field = (blocks, FINE + NEAR, LANES)
    halo = (blocks, FINE, LANES)
    coeffs, late, early, share_near, share_far, late_near, late_far, early_near, early_far = call(
        arrange_kernel, "arrange",
        [(4,) + field, (2,) + field, (2,) + field] + [(2,) + wide_field] * 2 + [(2,) + halo] * 4,
        landing + parts, start_field, guessed, diffusion, peclet_x, peclet_y, source, far=True, grant=61 * 2**20,
    )
    swap = [(i, i ^ 1) for i in range(strips)]
    cross = [(i, i + 1) for i in range(1, strips - 1, 2)] + [(i + 1, i) for i in range(1, strips - 1, 2)]
    mate = [(i, i ^ 1) for i in range(slabs)]

    def send(name, value, axis, route):
        with jax.named_scope(name):
            return lax.ppermute(value, axis, route)

    def exchange(name, near, far):
        return send(name + "_near", near, "space", swap), send(name + "_far", far, "space", cross)

    share_sides = exchange("share", share_near, share_far)
    late_sides = exchange("late", late_near, late_far)
    mates = send("mates", jnp.stack(share_sides), "tm", mate)
    early_sides = exchange("early", early_near, early_far)

    reach = 8 * -(-(SUBSTEPS * (2 * COARSEN_TWO - 1 + max(slabs - 3, 0))) // 8)
    spread = max(reach, NEAR)
    total = rows + 2 * (FINE + NEAR)
    window = (blocks, total + 2 * PAD, LANES)
    pair = [pltpu.VMEM((2,) + window, jnp.float32)] * 2
    work = 6 * 10**9
    near = (2, blocks, rows + 2 * NEAR, LANES)
    sent = [(2,) + field] + [(2,) + wide_field] * 2
    fine, raw, late_settled, late_near, late_far = call(
        open_kernel, "late_first_sweep",
        [(6,) + window, (3, blocks, rows + 2 * spread, LANES)] + sent,
        [pltpu.VMEM((4, blocks, total, LANES), jnp.float32)] + pair,
        coeffs, *share_sides, mates, late, *late_sides, cost=work,
    )
    late_sides = exchange("late_settled", late_near, late_far)
    early_settled, early_near, early_far = call(
        first_sweep, "early_first_sweep", sent, pair, fine, early, *early_sides, cost=work
    )
    early_sides = exchange("early_settled", early_near, early_far)
    (outgoing,) = call(
        late_kernel, "late_second_sweep", [(3,) + near[1:]], pair, fine, late_settled, *late_sides, cost=work
    )
    arrived = send("next_slab", outgoing, "tm", [(i, (i + 1) % slabs) for i in range(slabs)])
    settled, swept = call(
        early_kernel, "early_second_sweep", [near, near], pair, fine, early_settled, *early_sides, cost=work
    )
    padded = (blocks, rows + 2 * NEAR + 2 * PAD, LANES)
    e, c_value = call(
        slab_kernel, "slab_value", [(COARSEN_TWO,) + field, field],
        [pltpu.VMEM((5,) + padded, jnp.float32)] + [pltpu.VMEM((1,) + padded, jnp.float32)] * 2,
        raw, arrived, settled, swept, late_settled,
    )
    forward = [(i, i + 1) for i in range(strips - 1)]
    backward = [(i + 1, i) for i in range(strips - 1)]
    from_above = send("slab_down", c_value[:, rows - reach :, :], "space", forward)
    from_below = send("slab_up", c_value[:, :reach, :], "space", backward)
    gathered = lax.all_gather(c_value, "tm")
    edges = lax.all_gather(jnp.stack([from_above, from_below]), "tm")

    span = rows + 2 * reach
    wide = (blocks, span + 2 * PAD, LANES)
    plain = (slabs, blocks, span, LANES)
    out_parts = [pltpu.VMEM((COARSEN_TWO * rows, columns), jnp.bfloat16)] * 3
    (out,) = call(
        close_kernel, "close", [(COARSEN_TWO, rows, columns)],
        [pltpu.VMEM((5,) + wide, jnp.float32)] * 2
        + [pltpu.VMEM((slabs - 1,) + wide, jnp.float32)] * 2
        + [pltpu.VMEM(plain, jnp.float32)] * 2
        + [pltpu.VMEM((1,) + wide, jnp.float32)] * 2
        + out_parts,
        raw, gathered, edges, arrived, settled, late_settled, e,
    )
    return out


def solution(mesh):
    in_specs = (
        P("space", None),
        P("tm", "space", None),
        P("space", None),
        P("space", None),
        P("space", None),
        P("space", None),
    )
    out_specs = P("tm", "space", None)
    return jax.shard_map(
        on_device, mesh=mesh, in_specs=in_specs, out_specs=out_specs, check_vma=False
    )
```

```python
import functools

import jax
import jax.numpy as jnp
from jax import lax
from jax.experimental import pallas as pl
from jax.experimental.pallas import tpu as pltpu
from jax.sharding import PartitionSpec as P

SUBSTEPS = 4
COARSEN_ONE = 8
COARSEN_TWO = 4
LANES = 128
PAD = 8
NEAR = 16
FINE = SUBSTEPS * COARSEN_ONE
ALONE = 61 * 2**20
VMEM_LIMIT = 24 * 2**20


def is_last_slab():
    return lax.axis_index("tm") == lax.axis_size("tm") - 1


def vmem_specs(count):
    return [pl.BlockSpec(memory_space=pltpu.VMEM)] * count


def call(kernel, name, outs, scratch, *arrays, cost=0, far=False, grant=VMEM_LIMIT):
    held = [pl.BlockSpec(memory_space=pltpu.HBM)] * len(arrays) if far else vmem_specs(len(arrays))
    return pl.pallas_call(
        kernel,
        out_shape=[jax.ShapeDtypeStruct(shape, jnp.float32) for shape in outs],
        in_specs=held,
        out_specs=vmem_specs(len(outs)),
        scratch_shapes=scratch,
        name=name,
        compiler_params=pltpu.CompilerParams(vmem_limit_bytes=grant),
        cost_estimate=pl.CostEstimate(flops=cost, bytes_accessed=1 << 20, transcendentals=0),
    )(*arrays)


def column_order(columns, inverse):
    blocks = columns // LANES
    grid = lax.broadcasted_iota(jnp.int32, (columns, columns), 1 if inverse else 0)
    held = lax.broadcasted_iota(jnp.int32, (columns, columns), 0 if inverse else 1)
    matches = grid == (held % LANES) * blocks + held // LANES
    return jnp.where(matches, 1.0, 0.0).astype(jnp.bfloat16)


def split_three(value):
    high = value.astype(jnp.bfloat16)
    rest = value - high.astype(jnp.float32)
    middle = rest.astype(jnp.bfloat16)
    low = (rest - middle.astype(jnp.float32)).astype(jnp.bfloat16)
    return high, middle, low


def reorder(pieces, order):
    total = jnp.dot(pieces[2][...], order, preferred_element_type=jnp.float32)
    total = total + jnp.dot(pieces[1][...], order, preferred_element_type=jnp.float32)
    return total + jnp.dot(pieces[0][...], order, preferred_element_type=jnp.float32)


def substep(source, target, coeffs, low, high, points, with_source):
    blocks = source.shape[1]
    for row in range(low, high, 8):
        here = pl.ds(row, 8)
        centre = [[source[p, j, here, :] for j in range(blocks)] for p in range(points)]
        west_end = [pltpu.roll(centre[p][blocks - 1], 1, 1) for p in range(points)]
        east_end = [pltpu.roll(centre[p][0], LANES - 1, 1) for p in range(points)]
        for j in range(blocks):
            c = [coeffs[k, j, here, :] for k in range(6 if with_source else 5)]
            for p in range(points):
                west = west_end[p] if j == 0 else centre[p][j - 1]
                east = east_end[p] if j == blocks - 1 else centre[p][j + 1]
                north = source[p, j, pl.ds(row - 1, 8), :]
                south = source[p, j, pl.ds(row + 1, 8), :]
                own = c[0] * centre[p][j]
                if with_source:
                    own = own + c[5]
                target[p, j, here, :] = (own + (c[1] * north + c[2] * south)) + (
                    c[3] * west + c[4] * east
                )


def weights(raw, offset, coeffs, rows, scale, with_source):
    blocks = coeffs.shape[1]
    lane = lax.broadcasted_iota(jnp.int32, (8, LANES), 1)
    for j in range(blocks):
        for row in range(0, rows, 8):
            rate, along, across = (raw[k, j, pl.ds(offset + row, 8), :] for k in range(3))
            inverse = 1.0 / (1.0 + 4.0 * scale * rate)
            pull = scale * rate * inverse
            west = pull * (1.0 + along)
            east = pull * (1.0 - along)
            if j == 0:
                west = jnp.where(lane == 0, 0.0, west)
            if j == blocks - 1:
                east = jnp.where(lane == LANES - 1, 0.0, east)
            here = pl.ds(PAD + row, 8)
            coeffs[0, j, here, :] = inverse
            coeffs[1, j, here, :] = pull * (1.0 + across)
            coeffs[2, j, here, :] = pull * (1.0 - across)
            coeffs[3, j, here, :] = west
            coeffs[4, j, here, :] = east
            if with_source:
                coeffs[5, j, here, :] = scale * raw[3, j, pl.ds(offset + row, 8), :] * inverse


def clear_ends(ref):
    rows = ref.shape[2]
    edge = jnp.zeros(ref.shape[:2] + (PAD, LANES), jnp.float32)
    ref[:, :, 0:PAD, :] = edge
    ref[:, :, rows - PAD : rows, :] = edge


def sides(source, near, far):
    even = lax.axis_index("space") % 2 == 0
    rows = source.shape[-2]
    width = near.shape[-2]
    low = pl.multiple_of(jnp.where(even, rows - width, 0), 8)
    high = pl.multiple_of(jnp.where(even, 0, rows - width), 8)
    for k in range(near.shape[0]):
        near[k] = source[k, :, pl.ds(low, width), :]
        far[k] = source[k, :, pl.ds(high, width), :]


def arrange(sources, homes, landed, arrivals, parts):
    rows, columns = landed.shape[1:]
    blocks = columns // LANES
    copies = []
    for k, choices in enumerate(sources):
        made = [pltpu.make_async_copy(source, landed.at[k], arrivals.at[k]) for source in choices]
        copies.append(made[-1])
        if len(made) == 1:
            made[0].start()
        else:
            pl.when(is_last_slab())(made[0].start)
            pl.when(jnp.logical_not(is_last_slab()))(made[1].start)
    order = column_order(columns, False)
    for index, copy in enumerate(copies):
        copy.wait()
        for part, value in zip(parts, split_three(landed[index])):
            part[pl.ds(index * rows, rows), :] = value
    result = reorder(parts, order)
    for index, home in enumerate(homes):
        for j in range(blocks):
            home[j] = result[index * rows : (index + 1) * rows, j * LANES : (j + 1) * LANES]


def coeffs_kernel(rate, along, across, drive, coeffs, share_near, share_far, landed, arrivals, *parts):
    sources = [[rate], [along], [across], [drive]]
    arrange(sources, [coeffs.at[k] for k in range(4)], landed, arrivals, parts)
    sides(coeffs.at[pl.ds(2 * (lax.axis_index("tm") % 2), 2)], share_near, share_far)


def points_kernel(
    start, guessed, late, early, late_near, late_far, early_near, early_far, landed, arrivals, *parts
):
    sources = [[guessed.at[0]], [guessed.at[1]], [guessed.at[2]], [start, guessed.at[3]]]
    homes = [early.at[0], early.at[1], late.at[0], late.at[1]]
    arrange(sources, homes, landed, arrivals, parts)
    sides(late, late_near, late_far)
    sides(early, early_near, early_far)


def fill(window, base, own, near, far, targets):
    even = lax.axis_index("space") % 2 == 0
    rows = own.shape[2]
    width = near.shape[2]
    below = base + width + rows
    partner = pl.multiple_of(jnp.where(even, below, base), 8)
    other = pl.multiple_of(jnp.where(even, base, below), 8)
    for k, target in enumerate(targets):
        window[target, :, pl.ds(partner, width), :] = near[k]
        window[target, :, pl.ds(other, width), :] = far[k]


def run_sweep(a, b, coeffs, base, rows, points):
    for stage in range(FINE // 8):
        low = base + 8 * stage
        high = base + rows - 8 * stage

        def pairs(_, carry):
            for _ in range(2):
                substep(a, b, coeffs, low, high, points, True)
                substep(b, a, coeffs, low, high, points, True)
            return carry

        lax.fori_loop(0, 2, pairs, 0)


def window_kernel(own, near, far, a):
    a[...] = jnp.zeros(a.shape, jnp.float32)
    rows = own.shape[2]
    base = (a.shape[2] - rows) // 2 - near.shape[2]
    for p in range(own.shape[0]):
        a[p, :, pl.ds(base + near.shape[2], rows), :] = own[p]
    fill(a, base, own, near, far, range(own.shape[0]))


def load_points(a, b, own, near, far):
    points, _, rows, _ = own.shape
    width = near.shape[2]
    base = (a.shape[2] - rows) // 2 - width
    total = rows + 2 * width
    edge = jnp.zeros(a.shape[:2] + (PAD, LANES), jnp.float32)
    for ref in (a, b):
        ref[:, :, pl.ds(base - PAD, PAD), :] = edge
        ref[:, :, pl.ds(base + total, PAD), :] = edge
    for p in range(points):
        a[p, :, pl.ds(base + width, rows), :] = own[p]
    fill(a, base, own, near, far, range(points))
    return base, total


def first_sweep(coeffs, own, near, far, settled, next_near, next_far, a, b):
    base, total = load_points(a, b, own, near, far)
    run_sweep(a, b, coeffs, base, total, own.shape[0])
    settled[...] = a[:, :, pl.ds(base + FINE, own.shape[2]), :]
    sides(settled, next_near, next_far)


def open_kernel(
    mine, share_near, share_far, mates, loaded,
    coeffs, raw_out, settled, next_near, next_far, raw, a, b,
):
    rows = mine.shape[2]
    width = share_near.shape[2]
    total = rows + 2 * width
    for k in range(4):
        raw[k, :, pl.ds(width, rows), :] = mine[k]
    fill(raw, 0, mine, share_near, share_far, [2 * (lax.axis_index("tm") % 2) + k for k in range(2)])
    fill(raw, 0, mine, mates.at[0], mates.at[1], [2 - 2 * (lax.axis_index("tm") % 2) + k for k in range(2)])
    weights(raw, 0, coeffs, total, 1.0, True)
    clear_ends(coeffs)
    raw_rows = raw_out.shape[2]
    raw_out[...] = raw[0:3, :, pl.ds((total - raw_rows) // 2, raw_rows), :]
    a[...] = loaded[...]
    b[...] = loaded[...]
    run_sweep(a, b, coeffs, PAD + NEAR, rows + 2 * FINE, a.shape[0])
    settled[...] = a[:, :, pl.ds(PAD + NEAR + FINE, rows), :]
    sides(settled, next_near, next_far)


def second_sweep(coeffs, own, near, far, a, b):
    base, total = load_points(a, b, own, near, far)
    keep = pl.ds(base + FINE, total - 2 * FINE)
    return base, total, keep


def moved(packed, rows):
    ends = (rows + 2 * NEAR, 2 * rows + 3 * NEAR, 3 * rows + 3 * NEAR)
    starts = (0,) + ends[:2]
    return [packed.at[:, pl.ds(start, end - start), :] for start, end in zip(starts, ends)]


def late_kernel(coeffs, own, near, far, shift_out, a, b):
    base, total, keep = second_sweep(coeffs, own, near, far, a, b)
    rows = own.shape[2]
    residual, swept, settled = moved(shift_out, rows)
    settled[...] = own[1]
    before = a[1, :, keep, :]
    residual[...] = before
    run_sweep(a, b, coeffs, base, total, own.shape[0])
    swept[...] = a[1, :, pl.ds(base + FINE + NEAR // 2, rows + NEAR), :]

    @pl.when(is_last_slab())
    def _():
        residual[...] = residual[...] - residual[...]

    @pl.when(jnp.logical_not(is_last_slab()))
    def _():
        residual[...] = a[0, :, keep, :] - residual[...]


def early_kernel(coeffs, own, near, far, settled_out, swept_out, a, b):
    base, total, keep = second_sweep(coeffs, own, near, far, a, b)
    settled_out[...] = a[:, :, keep, :]
    run_sweep(a, b, coeffs, base, total, own.shape[0])
    swept_out[...] = a[:, :, keep, :]


def coarse_step(a, b, coeffs, reach, rows, points):
    own = (a.shape[2] - rows) // 2
    for step in range(SUBSTEPS):
        source, target = (a, b) if step % 2 == 0 else (b, a)
        halo = 8 * -(-(reach - step - 1) // 8)
        substep(source, target, coeffs, own - halo, own + rows + halo, points, False)


def slab_kernel(raw, arrived, settled, swept, settled_last, e_out, c_out, c_near, c_far, coeffs, a, b):
    kept = settled.shape[2]
    rows = settled_last.shape[2]
    weights(raw, (raw.shape[2] - kept) // 2, coeffs, kept, float(COARSEN_ONE), False)
    for ref in (a, b):
        clear_ends(ref)
    inner = pl.ds(PAD, kept)
    own = pl.ds(NEAR, rows)
    held = pl.ds(PAD + NEAR, rows)
    first, second, _ = moved(arrived, rows)
    trimmed = pl.ds(PAD + NEAR // 2, rows + NEAR)
    a[0, :, inner, :] = first[...]
    e_out[0] = a[0, :, held, :]
    for position in range(1, COARSEN_TWO):
        coarse_step(a, b, coeffs, SUBSTEPS * (COARSEN_TWO - position), rows, 1)
        if position == 1:
            value = second[...] - settled[0, :, pl.ds(NEAR // 2, rows + NEAR), :]
            a[0, :, trimmed, :] = a[0, :, trimmed, :] + value
        elif position == 2:
            a[0, :, inner, :] = a[0, :, inner, :] + (swept[0] - settled[1])
        else:
            a[0, :, held, :] = a[0, :, held, :] + (swept[1, :, own, :] - settled_last[0])
        e_out[position] = a[0, :, held, :]
    c_out[0] = e_out[COARSEN_TWO - 1]
    sides(c_out, c_near, c_far)


def close_kernel(raw, gathered, edges, arrived, settled, settled_last, e, out, level_coeffs, top_coeffs, a, b, w, l, x, y, *parts):
    even = lax.axis_index("space") % 2 == 0
    slabs = gathered.shape[0]
    chain = slabs - 1
    rows = gathered.shape[2]
    reach = edges.shape[3]
    total = rows + 2 * reach
    offset = (raw.shape[2] - total) // 2
    weights(raw, offset, level_coeffs, total, float(COARSEN_ONE), False)
    weights(raw, offset, top_coeffs, total, float(COARSEN_ONE * COARSEN_TWO), False)
    for ref in (a, b, x, y):
        clear_ends(ref)
    for k in range(chain):
        a[k, :, pl.ds(PAD + reach, rows), :] = gathered[k]
        low, high = PAD, PAD + reach + rows
        partner = pl.multiple_of(jnp.where(even, high, low), 8)
        other = pl.multiple_of(jnp.where(even, low, high), 8)
        a[k, :, pl.ds(partner, reach), :] = edges[k, 0]
        a[k, :, pl.ds(other, reach), :] = edges[k, 1]
    inner = pl.ds(PAD, total)
    w[0] = jnp.zeros(w.shape[1:], jnp.float32)
    l[0] = jnp.zeros(l.shape[1:], jnp.float32)
    for k in range(chain):
        w[k + 1] = a[k, :, inner, :]
    for step in range(COARSEN_TWO):
        coarse_step(a, b, level_coeffs, reach - step * SUBSTEPS, rows, chain)
    left = reach - COARSEN_TWO * SUBSTEPS
    x[0, :, inner, :] = a[0, :, inner, :]
    l[1] = x[0, :, inner, :]
    for k in range(1, chain):
        w[k + 1] = w[k + 1] + l[k]
        coarse_step(x, y, top_coeffs, left if k < chain - 1 else SUBSTEPS, rows, 1)
        left -= SUBSTEPS
        x[0, :, inner, :] = x[0, :, inner, :] + a[k, :, inner, :]
        l[k + 1] = x[0, :, inner, :]
    slab = lax.axis_index("tm")
    own = pl.ds(reach, rows)
    held = pl.ds(PAD + reach, rows)
    x[0, :, inner, :] = w[slab]
    blocks = gathered.shape[1]
    for position in range(COARSEN_TWO):
        if position < COARSEN_TWO - 1:
            coarse_step(x, y, level_coeffs, SUBSTEPS * (COARSEN_TWO - 1 - position), rows, 1)
            if position == 0:
                settled_here = moved(arrived, rows)[2]
            else:
                settled_here = settled.at[position - 1, :, pl.ds(NEAR, rows), :]
            value = x[0, :, held, :]
        else:
            settled_here = settled_last.at[0]
            value = l[slab, :, own, :]
        value = (settled_here[...] + e[position]) + value
        for j in range(blocks):
            for part, piece in zip(parts, split_three(value[j])):
                part[pl.ds(position * rows, rows), j * LANES : (j + 1) * LANES] = piece
    result = reorder(parts, column_order(blocks * LANES, True))
    for position in range(COARSEN_TWO):
        out[position] = result[position * rows : (position + 1) * rows]


def on_device(start_field, guessed, diffusion, peclet_x, peclet_y, source):
    points, rows, columns = guessed.shape
    blocks = columns // LANES
    slabs = lax.axis_size("tm")
    strips = lax.axis_size("space")

    field = (blocks, rows, LANES)
    wide_field = (blocks, FINE + NEAR, LANES)
    halo = (blocks, FINE, LANES)
    landing = [pltpu.VMEM((4, rows, columns), jnp.float32), pltpu.SemaphoreType.DMA((4,))]
    parts = [pltpu.VMEM((4 * rows, columns), jnp.bfloat16)] * 3
    coeffs, share_near, share_far = call(
        coeffs_kernel, "arrange_coeffs", [(4,) + field] + [(2,) + wide_field] * 2,
        landing + parts, diffusion, peclet_x, peclet_y, source, far=True, grant=ALONE,
    )
    late, early, late_near, late_far, early_near, early_far = call(
        points_kernel, "arrange_points", [(2,) + field] * 2 + [(2,) + halo] * 4,
        landing + parts, start_field, guessed, cost=2 * 10**9, far=True,
    )
    swap = [(i, i ^ 1) for i in range(strips)]
    cross = [(i, i + 1) for i in range(1, strips - 1, 2)] + [(i + 1, i) for i in range(1, strips - 1, 2)]
    mate = [(i, i ^ 1) for i in range(slabs)]

    def send(name, value, axis, route):
        with jax.named_scope(name):
            return lax.ppermute(value, axis, route)

    def exchange(name, near, far):
        return send(name + "_near", near, "space", swap), send(name + "_far", far, "space", cross)

    share_sides = exchange("share", share_near, share_far)
    late_sides = exchange("late", late_near, late_far)
    mates = send("mates", jnp.stack(share_sides), "tm", mate)
    early_near, early_far, _ = lax.optimization_barrier((early_near, early_far, share_sides[0]))
    early_sides = exchange("early", early_near, early_far)

    reach = 8 * -(-(SUBSTEPS * (2 * COARSEN_TWO - 1 + max(slabs - 3, 0))) // 8)
    spread = max(reach, NEAR)
    total = rows + 2 * (FINE + NEAR)
    window = (blocks, total + 2 * PAD, LANES)
    pair = [pltpu.VMEM((2,) + window, jnp.float32)] * 2
    work = 6 * 10**9
    near = (2, blocks, rows + 2 * NEAR, LANES)
    sent = [(2,) + field] + [(2,) + wide_field] * 2
    (loaded,) = call(window_kernel, "late_window", [(2,) + window], [], late, *late_sides, cost=10 * 10**9)
    fine, raw, late_settled, late_near, late_far = call(
        open_kernel, "late_first_sweep",
        [(6,) + window, (3, blocks, rows + 2 * spread, LANES)] + sent,
        [pltpu.VMEM((4, blocks, total, LANES), jnp.float32)] + pair,
        coeffs, *share_sides, mates, loaded, cost=10**9,
    )
    late_sides = exchange("late_settled", late_near, late_far)
    early_settled, early_near, early_far = call(
        first_sweep, "early_first_sweep", sent, pair, fine, early, *early_sides, cost=work
    )
    early_sides = exchange("early_settled", early_near, early_far)
    (outgoing,) = call(
        late_kernel, "late_second_sweep", [(blocks, 3 * (rows + NEAR), LANES)], pair, fine, late_settled, *late_sides, cost=work
    )
    arrived = send("next_slab", outgoing, "tm", [(i, (i + 1) % slabs) for i in range(slabs)])
    settled, swept = call(
        early_kernel, "early_second_sweep", [near, near], pair, fine, early_settled, *early_sides, cost=work
    )
    padded = (blocks, rows + 2 * NEAR + 2 * PAD, LANES)
    e, c_value, c_near, c_far = call(
        slab_kernel, "slab_value", [(COARSEN_TWO,) + field, (1,) + field] + [(1, blocks, reach, LANES)] * 2,
        [pltpu.VMEM((5,) + padded, jnp.float32)] + [pltpu.VMEM((1,) + padded, jnp.float32)] * 2,
        raw, arrived, settled, swept, late_settled,
    )
    c_sides = exchange("slab", c_near, c_far)
    gathered = lax.all_gather(c_value[0], "tm")
    edges = lax.all_gather(jnp.concatenate(c_sides), "tm")

    span = rows + 2 * reach
    wide = (blocks, span + 2 * PAD, LANES)
    plain = (slabs, blocks, span, LANES)
    out_parts = [pltpu.VMEM((COARSEN_TWO * rows, columns), jnp.bfloat16)] * 3
    (out,) = call(
        close_kernel, "close", [(COARSEN_TWO, rows, columns)],
        [pltpu.VMEM((5,) + wide, jnp.float32)] * 2
        + [pltpu.VMEM((slabs - 1,) + wide, jnp.float32)] * 2
        + [pltpu.VMEM(plain, jnp.float32)] * 2
        + [pltpu.VMEM((1,) + wide, jnp.float32)] * 2
        + out_parts,
        raw, gathered, edges, arrived, settled, late_settled, e,
    )
    return out


def solution(mesh):
    in_specs = (
        P("space", None),
        P("tm", "space", None),
        P("space", None),
        P("space", None),
        P("space", None),
        P("space", None),
    )
    out_specs = P("tm", "space", None)
    return jax.shard_map(
        on_device, mesh=mesh, in_specs=in_specs, out_specs=out_specs, check_vma=False
    )
```

```python
import functools

import jax
import jax.numpy as jnp
from jax import lax
from jax.experimental import pallas as pl
from jax.experimental.pallas import tpu as pltpu
from jax.sharding import PartitionSpec as P

SUBSTEPS = 4
COARSEN_ONE = 8
COARSEN_TWO = 4
LANES = 128
PAD = 8
NEAR = 16
FINE = SUBSTEPS * COARSEN_ONE
VMEM_LIMIT = 24 * 2**20


def is_last_slab():
    return lax.axis_index("tm") == lax.axis_size("tm") - 1


def vmem_specs(count):
    return [pl.BlockSpec(memory_space=pltpu.VMEM)] * count


def call(kernel, name, outs, scratch, *arrays, cost=0):
    return pl.pallas_call(
        kernel,
        out_shape=[jax.ShapeDtypeStruct(shape, jnp.float32) for shape in outs],
        in_specs=vmem_specs(len(arrays)),
        out_specs=vmem_specs(len(outs)),
        scratch_shapes=scratch,
        name=name,
        compiler_params=pltpu.CompilerParams(vmem_limit_bytes=VMEM_LIMIT),
        cost_estimate=pl.CostEstimate(flops=cost, bytes_accessed=1 << 20, transcendentals=0),
    )(*arrays)


def column_order(columns, inverse):
    blocks = columns // LANES
    grid = lax.broadcasted_iota(jnp.int32, (columns, columns), 1 if inverse else 0)
    held = lax.broadcasted_iota(jnp.int32, (columns, columns), 0 if inverse else 1)
    matches = grid == (held % LANES) * blocks + held // LANES
    return jnp.where(matches, 1.0, 0.0).astype(jnp.bfloat16)


def split_three(value):
    high = value.astype(jnp.bfloat16)
    rest = value - high.astype(jnp.float32)
    middle = rest.astype(jnp.bfloat16)
    low = (rest - middle.astype(jnp.float32)).astype(jnp.bfloat16)
    return high, middle, low


def reorder(pieces, order):
    total = jnp.dot(pieces[2][...], order, preferred_element_type=jnp.float32)
    total = total + jnp.dot(pieces[1][...], order, preferred_element_type=jnp.float32)
    return total + jnp.dot(pieces[0][...], order, preferred_element_type=jnp.float32)


def substep(source, target, coeffs, low, high, points, with_source):
    blocks = source.shape[1]
    for row in range(low, high, 8):
        here = pl.ds(row, 8)
        centre = [[source[p, j, here, :] for j in range(blocks)] for p in range(points)]
        west_end = [pltpu.roll(centre[p][blocks - 1], 1, 1) for p in range(points)]
        east_end = [pltpu.roll(centre[p][0], LANES - 1, 1) for p in range(points)]
        for j in range(blocks):
            c = [coeffs[k, j, here, :] for k in range(6 if with_source else 5)]
            for p in range(points):
                west = west_end[p] if j == 0 else centre[p][j - 1]
                east = east_end[p] if j == blocks - 1 else centre[p][j + 1]
                north = source[p, j, pl.ds(row - 1, 8), :]
                south = source[p, j, pl.ds(row + 1, 8), :]
                own = c[0] * centre[p][j]
                if with_source:
                    own = own + c[5]
                target[p, j, here, :] = (own + (c[1] * north + c[2] * south)) + (
                    c[3] * west + c[4] * east
                )


def weights(raw, offset, coeffs, rows, scale, with_source):
    blocks = coeffs.shape[1]
    lane = lax.broadcasted_iota(jnp.int32, (8, LANES), 1)
    for j in range(blocks):
        for row in range(0, rows, 8):
            rate, along, across = (raw[k, j, pl.ds(offset + row, 8), :] for k in range(3))
            inverse = 1.0 / (1.0 + 4.0 * scale * rate)
            pull = scale * rate * inverse
            west = pull * (1.0 + along)
            east = pull * (1.0 - along)
            if j == 0:
                west = jnp.where(lane == 0, 0.0, west)
            if j == blocks - 1:
                east = jnp.where(lane == LANES - 1, 0.0, east)
            here = pl.ds(PAD + row, 8)
            coeffs[0, j, here, :] = inverse
            coeffs[1, j, here, :] = pull * (1.0 + across)
            coeffs[2, j, here, :] = pull * (1.0 - across)
            coeffs[3, j, here, :] = west
            coeffs[4, j, here, :] = east
            if with_source:
                coeffs[5, j, here, :] = scale * raw[3, j, pl.ds(offset + row, 8), :] * inverse


def clear_ends(ref):
    rows = ref.shape[2]
    edge = jnp.zeros(ref.shape[:2] + (PAD, LANES), jnp.float32)
    ref[:, :, 0:PAD, :] = edge
    ref[:, :, rows - PAD : rows, :] = edge


def sides(source, near, far):
    even = lax.axis_index("space") % 2 == 0
    rows = source.shape[-2]
    width = near.shape[-2]
    low = pl.multiple_of(jnp.where(even, rows - width, 0), 8)
    high = pl.multiple_of(jnp.where(even, 0, rows - width), 8)
    for k in range(near.shape[0]):
        near[k] = source[k, :, pl.ds(low, width), :]
        far[k] = source[k, :, pl.ds(high, width), :]


def arrange(fields, homes, parts):
    count, rows, columns = fields.shape
    for index in range(count):
        for part, value in zip(parts, split_three(fields[index])):
            part[pl.ds(index * rows, rows), :] = value
    result = reorder(parts, column_order(columns, False))
    for index, home in enumerate(homes):
        for j in range(columns // LANES):
            home[j] = result[index * rows : (index + 1) * rows, j * LANES : (j + 1) * LANES]


def coeffs_kernel(fields, coeffs, share_near, share_far, *parts):
    arrange(fields, [coeffs.at[k] for k in range(4)], parts)
    sides(coeffs.at[pl.ds(2 * (lax.axis_index("tm") % 2), 2)], share_near, share_far)


def points_kernel(fields, late, early, late_near, late_far, early_near, early_far, *parts):
    arrange(fields, [early.at[0], early.at[1], late.at[0], late.at[1]], parts)
    sides(late, late_near, late_far)
    sides(early, early_near, early_far)


def fill(window, base, own, near, far, targets):
    even = lax.axis_index("space") % 2 == 0
    rows = own.shape[2]
    width = near.shape[2]
    below = base + width + rows
    partner = pl.multiple_of(jnp.where(even, below, base), 8)
    other = pl.multiple_of(jnp.where(even, base, below), 8)
    for k, target in enumerate(targets):
        window[target, :, pl.ds(partner, width), :] = near[k]
        window[target, :, pl.ds(other, width), :] = far[k]


def run_sweep(a, b, coeffs, base, rows, points):
    for stage in range(FINE // 8):
        low = base + 8 * stage
        high = base + rows - 8 * stage

        def pairs(_, carry):
            for _ in range(2):
                substep(a, b, coeffs, low, high, points, True)
                substep(b, a, coeffs, low, high, points, True)
            return carry

        lax.fori_loop(0, 2, pairs, 0)


def window_kernel(own, near, far, a):
    a[...] = jnp.zeros(a.shape, jnp.float32)
    rows = own.shape[2]
    base = (a.shape[2] - rows) // 2 - near.shape[2]
    for p in range(own.shape[0]):
        a[p, :, pl.ds(base + near.shape[2], rows), :] = own[p]
    fill(a, base, own, near, far, range(own.shape[0]))


def load_points(a, b, own, near, far):
    points, _, rows, _ = own.shape
    width = near.shape[2]
    base = (a.shape[2] - rows) // 2 - width
    total = rows + 2 * width
    edge = jnp.zeros(a.shape[:2] + (PAD, LANES), jnp.float32)
    for ref in (a, b):
        ref[:, :, pl.ds(base - PAD, PAD), :] = edge
        ref[:, :, pl.ds(base + total, PAD), :] = edge
    for p in range(points):
        a[p, :, pl.ds(base + width, rows), :] = own[p]
    fill(a, base, own, near, far, range(points))
    return base, total


def first_sweep(coeffs, own, near, far, settled, next_near, next_far, a, b):
    base, total = load_points(a, b, own, near, far)
    run_sweep(a, b, coeffs, base, total, own.shape[0])
    settled[...] = a[:, :, pl.ds(base + FINE, own.shape[2]), :]
    sides(settled, next_near, next_far)


def open_kernel(
    mine, share_near, share_far, mates, loaded,
    coeffs, raw_out, settled, next_near, next_far, raw, a, b,
):
    rows = mine.shape[2]
    width = share_near.shape[2]
    total = rows + 2 * width
    for k in range(4):
        raw[k, :, pl.ds(width, rows), :] = mine[k]
    fill(raw, 0, mine, share_near, share_far, [2 * (lax.axis_index("tm") % 2) + k for k in range(2)])
    fill(raw, 0, mine, mates.at[0], mates.at[1], [2 - 2 * (lax.axis_index("tm") % 2) + k for k in range(2)])
    weights(raw, 0, coeffs, total, 1.0, True)
    clear_ends(coeffs)
    raw_rows = raw_out.shape[2]
    raw_out[...] = raw[0:3, :, pl.ds((total - raw_rows) // 2, raw_rows), :]
    a[...] = loaded[...]
    b[...] = loaded[...]
    run_sweep(a, b, coeffs, PAD + NEAR, rows + 2 * FINE, a.shape[0])
    settled[...] = a[:, :, pl.ds(PAD + NEAR + FINE, rows), :]
    sides(settled, next_near, next_far)


def second_sweep(coeffs, own, near, far, a, b):
    base, total = load_points(a, b, own, near, far)
    keep = pl.ds(base + FINE, total - 2 * FINE)
    return base, total, keep


def moved(packed, rows):
    ends = (rows + 2 * NEAR, 2 * rows + 3 * NEAR, 3 * rows + 3 * NEAR)
    starts = (0,) + ends[:2]
    return [packed.at[:, pl.ds(start, end - start), :] for start, end in zip(starts, ends)]


def late_kernel(coeffs, own, near, far, shift_out, a, b):
    base, total, keep = second_sweep(coeffs, own, near, far, a, b)
    rows = own.shape[2]
    residual, swept, settled = moved(shift_out, rows)
    settled[...] = own[1]
    before = a[1, :, keep, :]
    residual[...] = before
    run_sweep(a, b, coeffs, base, total, own.shape[0])
    swept[...] = a[1, :, pl.ds(base + FINE + NEAR // 2, rows + NEAR), :]

    @pl.when(is_last_slab())
    def _():
        residual[...] = residual[...] - residual[...]

    @pl.when(jnp.logical_not(is_last_slab()))
    def _():
        residual[...] = a[0, :, keep, :] - residual[...]


def early_kernel(coeffs, own, near, far, settled_out, swept_out, a, b):
    base, total, keep = second_sweep(coeffs, own, near, far, a, b)
    settled_out[...] = a[:, :, keep, :]
    run_sweep(a, b, coeffs, base, total, own.shape[0])
    swept_out[...] = a[:, :, keep, :]


def coarse_step(a, b, coeffs, reach, rows, points):
    own = (a.shape[2] - rows) // 2
    for step in range(SUBSTEPS):
        source, target = (a, b) if step % 2 == 0 else (b, a)
        halo = 8 * -(-(reach - step - 1) // 8)
        substep(source, target, coeffs, own - halo, own + rows + halo, points, False)


def slab_kernel(raw, arrived, settled, swept, settled_last, e_out, c_out, c_near, c_far, coeffs, a, b):
    rows = settled_last.shape[2]
    kept = rows + 2 * NEAR
    weights(raw, (raw.shape[2] - kept) // 2, coeffs, kept, float(COARSEN_ONE), False)
    for ref in (a, b):
        clear_ends(ref)
    inner = pl.ds(PAD, kept)
    own = pl.ds(NEAR // 2, rows)
    held = pl.ds(PAD + NEAR, rows)
    first, second, _ = moved(arrived, rows)
    trimmed = pl.ds(PAD + NEAR // 2, rows + NEAR)
    a[0, :, inner, :] = first[...]
    e_out[0] = a[0, :, held, :]
    for position in range(1, COARSEN_TWO):
        coarse_step(a, b, coeffs, SUBSTEPS * (COARSEN_TWO - position), rows, 1)
        if position == 1:
            a[0, :, trimmed, :] = a[0, :, trimmed, :] + (second[...] - settled[0])
        elif position == 2:
            a[0, :, trimmed, :] = a[0, :, trimmed, :] + (swept[0] - settled[1])
        else:
            a[0, :, held, :] = a[0, :, held, :] + (swept[1, :, own, :] - settled_last[0])
        e_out[position] = a[0, :, held, :]
    c_out[0] = e_out[COARSEN_TWO - 1]
    sides(c_out, c_near, c_far)


def close_kernel(raw, gathered, edges, arrived, settled, settled_last, e, out, level_coeffs, top_coeffs, a, b, w, l, x, y, *parts):
    even = lax.axis_index("space") % 2 == 0
    slabs = gathered.shape[0]
    chain = slabs - 1
    rows = gathered.shape[2]
    reach = edges.shape[3]
    total = rows + 2 * reach
    offset = (raw.shape[2] - total) // 2
    weights(raw, offset, level_coeffs, total, float(COARSEN_ONE), False)
    weights(raw, offset, top_coeffs, total, float(COARSEN_ONE * COARSEN_TWO), False)
    for ref in (a, b, x, y):
        clear_ends(ref)
    for k in range(chain):
        a[k, :, pl.ds(PAD + reach, rows), :] = gathered[k]
        low, high = PAD, PAD + reach + rows
        partner = pl.multiple_of(jnp.where(even, high, low), 8)
        other = pl.multiple_of(jnp.where(even, low, high), 8)
        a[k, :, pl.ds(partner, reach), :] = edges[k, 0]
        a[k, :, pl.ds(other, reach), :] = edges[k, 1]
    inner = pl.ds(PAD, total)
    w[0] = jnp.zeros(w.shape[1:], jnp.float32)
    l[0] = jnp.zeros(l.shape[1:], jnp.float32)
    for k in range(chain):
        w[k + 1] = a[k, :, inner, :]
    for step in range(COARSEN_TWO):
        coarse_step(a, b, level_coeffs, reach - step * SUBSTEPS, rows, chain)
    left = reach - COARSEN_TWO * SUBSTEPS
    x[0, :, inner, :] = a[0, :, inner, :]
    l[1] = x[0, :, inner, :]
    for k in range(1, chain):
        w[k + 1] = w[k + 1] + l[k]
        coarse_step(x, y, top_coeffs, left if k < chain - 1 else SUBSTEPS, rows, 1)
        left -= SUBSTEPS
        x[0, :, inner, :] = x[0, :, inner, :] + a[k, :, inner, :]
        l[k + 1] = x[0, :, inner, :]
    slab = lax.axis_index("tm")
    own = pl.ds(reach, rows)
    held = pl.ds(PAD + reach, rows)
    x[0, :, inner, :] = w[slab]
    blocks = gathered.shape[1]
    for position in range(COARSEN_TWO):
        if position < COARSEN_TWO - 1:
            coarse_step(x, y, level_coeffs, SUBSTEPS * (COARSEN_TWO - 1 - position), rows, 1)
            if position == 0:
                settled_here = moved(arrived, rows)[2]
            else:
                settled_here = settled.at[position - 1, :, pl.ds(NEAR // 2, rows), :]
            value = x[0, :, held, :]
        else:
            settled_here = settled_last.at[0]
            value = l[slab, :, own, :]
        value = (settled_here[...] + e[position]) + value
        for j in range(blocks):
            for part, piece in zip(parts, split_three(value[j])):
                part[pl.ds(position * rows, rows), j * LANES : (j + 1) * LANES] = piece
    result = reorder(parts, column_order(blocks * LANES, True))
    for position in range(COARSEN_TWO):
        out[position] = result[position * rows : (position + 1) * rows]


def on_device(start_field, guessed, diffusion, peclet_x, peclet_y, source):
    points, rows, columns = guessed.shape
    blocks = columns // LANES
    slabs = lax.axis_size("tm")
    strips = lax.axis_size("space")

    field = (blocks, rows, LANES)
    wide_field = (blocks, FINE + NEAR, LANES)
    halo = (blocks, FINE, LANES)
    closing = jnp.where(is_last_slab(), start_field, guessed[points - 1])
    fields = jnp.concatenate([guessed[: points - 1], closing[None]])
    parts = [pltpu.VMEM((4 * rows, columns), jnp.bfloat16)] * 3
    coeffs, share_near, share_far = call(
        coeffs_kernel, "arrange_coeffs", [(4,) + field] + [(2,) + wide_field] * 2,
        parts, jnp.stack([diffusion, peclet_x, peclet_y, source]),
    )
    late, early, late_near, late_far, early_near, early_far = call(
        points_kernel, "arrange_points", [(2,) + field] * 2 + [(2,) + halo] * 4,
        parts, fields, cost=2 * 10**9,
    )
    swap = [(i, i ^ 1) for i in range(strips)]
    cross = [(i, i + 1) for i in range(1, strips - 1, 2)] + [(i + 1, i) for i in range(1, strips - 1, 2)]
    mate = [(i, i ^ 1) for i in range(slabs)]

    def send(name, value, axis, route):
        with jax.named_scope(name):
            return lax.ppermute(value, axis, route)

    def exchange(name, near, far):
        return send(name + "_near", near, "space", swap), send(name + "_far", far, "space", cross)

    share_sides = exchange("share", share_near, share_far)
    late_sides = exchange("late", late_near, late_far)
    mates = send("mates", jnp.stack(share_sides), "tm", mate)
    early_near, early_far, _ = lax.optimization_barrier((early_near, early_far, share_sides[0]))
    early_sides = exchange("early", early_near, early_far)

    reach = 8 * -(-(SUBSTEPS * (2 * COARSEN_TWO - 1 + max(slabs - 3, 0))) // 8)
    spread = max(reach, NEAR)
    total = rows + 2 * (FINE + NEAR)
    window = (blocks, total + 2 * PAD, LANES)
    pair = [pltpu.VMEM((2,) + window, jnp.float32)] * 2
    work = 6 * 10**9
    near = (2, blocks, rows + NEAR, LANES)
    sent = [(2,) + field] + [(2,) + wide_field] * 2
    sent_early = [(2,) + field] + [(2, blocks, FINE + NEAR // 2, LANES)] * 2
    (loaded,) = call(window_kernel, "late_window", [(2,) + window], [], late, *late_sides, cost=10 * 10**9)
    fine, raw, late_settled, late_near, late_far = call(
        open_kernel, "late_first_sweep",
        [(6,) + window, (3, blocks, rows + 2 * spread, LANES)] + sent,
        [pltpu.VMEM((4, blocks, total, LANES), jnp.float32)] + pair,
        coeffs, *share_sides, mates, loaded, cost=10**9,
    )
    late_sides = exchange("late_settled", late_near, late_far)
    early_settled, early_near, early_far = call(
        first_sweep, "early_first_sweep", sent_early, pair, fine, early, *early_sides, cost=work
    )
    early_sides = exchange("early_settled", early_near, early_far)
    (outgoing,) = call(
        late_kernel, "late_second_sweep", [(blocks, 3 * (rows + NEAR), LANES)], pair, fine, late_settled, *late_sides, cost=work
    )
    arrived = send("next_slab", outgoing, "tm", [(i, (i + 1) % slabs) for i in range(slabs)])
    settled, swept = call(
        early_kernel, "early_second_sweep", [near, near], pair, fine, early_settled, *early_sides, cost=work
    )
    padded = (blocks, rows + 2 * NEAR + 2 * PAD, LANES)
    e, c_value, c_near, c_far = call(
        slab_kernel, "slab_value", [(COARSEN_TWO,) + field, (1,) + field] + [(1, blocks, reach, LANES)] * 2,
        [pltpu.VMEM((5,) + padded, jnp.float32)] + [pltpu.VMEM((1,) + padded, jnp.float32)] * 2,
        raw, arrived, settled, swept, late_settled,
    )
    c_sides = exchange("slab", c_near, c_far)
    gathered = lax.all_gather(c_value[0], "tm")
    edges = lax.all_gather(jnp.concatenate(c_sides), "tm")

    span = rows + 2 * reach
    wide = (blocks, span + 2 * PAD, LANES)
    plain = (slabs, blocks, span, LANES)
    out_parts = [pltpu.VMEM((COARSEN_TWO * rows, columns), jnp.bfloat16)] * 3
    (out,) = call(
        close_kernel, "close", [(COARSEN_TWO, rows, columns)],
        [pltpu.VMEM((5,) + wide, jnp.float32)] * 2
        + [pltpu.VMEM((slabs - 1,) + wide, jnp.float32)] * 2
        + [pltpu.VMEM(plain, jnp.float32)] * 2
        + [pltpu.VMEM((1,) + wide, jnp.float32)] * 2
        + out_parts,
        raw, gathered, edges, arrived, settled, late_settled, e,
    )
    return out


def solution(mesh):
    in_specs = (
        P("space", None),
        P("tm", "space", None),
        P("space", None),
        P("space", None),
        P("space", None),
        P("space", None),
    )
    out_specs = P("tm", "space", None)
    return jax.shard_map(
        on_device, mesh=mesh, in_specs=in_specs, out_specs=out_specs, check_vma=False
    )
```
